512 devices in a mesh: seq: 32 (over z, x), tp: 16 (over y, core).
Axes of the slice: x: 4, y: 8, z: 8, core: 2. Of those that a mesh axis runs over, the one named last changes fastest.
Arguments:
- queries: bfloat16 [16384, 4096], P('seq', 'tp'), may hold values from -12 to 12
- keys: bfloat16 [16384, 4096], P('seq', 'tp'), may hold values from -6 to 6
- values: bfloat16 [16384, 4096], P('seq', 'tp'), may hold values from -6 to 6
- gain: bfloat16 [4096], P('tp'), may hold values from 0.25 to 1.75
- grad_out: bfloat16 [16384, 4096], P('seq', 'tp'), may hold values from -6 to 6
Outputs:
- grad_queries: bfloat16 [16384, 4096], P('seq', 'tp')
- grad_keys: bfloat16 [16384, 4096], P('seq', 'tp')
- grad_values: bfloat16 [16384, 4096], P('seq', 'tp')
The draws below stay inside these ranges and needn't reach their ends.
All inputs are finite; a program needn't handle non-finite values.
Results may differ from the reference program's by a relative error of at most 0.0058.
Values sent between devices are 32-bit elements; how exact they have to be, the bound alone decides.
No kernel may reach another device: no remote copies, remote signals or barrier semaphores. Data moves between devices by JAX's collectives and lax.ppermute only.
A program may use at most 64 MiB of HBM per device.

```python
import jax
import jax.numpy as jnp
from jax import lax

H = 32
HD = 128
D = 4096
BLK = 512
TOKENS = 16384


def draw_queries(key, part):
    key = jax.random.fold_in(key, 7)
    head = (jnp.arange(H * HD) // HD).astype(jnp.float32)
    base = jnp.clip(jax.random.normal(key, (TOKENS, H * HD), jnp.float32), -4.0, 4.0)
    rise = 3.0 ** (head / (H - 1))
    return (base * rise[None, :]).astype(jnp.bfloat16)


def level_of(own_key, shape, cuts, smallest, high):
    factor_of = 1.0
    for axis_at, shards_of in cuts:
        steps = jax.random.uniform(jax.random.fold_in(jax.random.fold_in(own_key, 6), axis_at), (shards_of,), jnp.float32, smallest / len(cuts), high / len(cuts))
        factor_of = factor_of * jnp.repeat(jnp.exp(steps), shape[axis_at] // shards_of).reshape((-1,) + (1,) * (len(shape) - 1 - axis_at))
    return factor_of


def bell_draw(own_key, extent, scale, limit, pieces=(), kind=jnp.bfloat16):
    drawn = scale * jax.random.normal(own_key, extent, jnp.float32)
    if pieces:
        drawn = drawn * level_of(own_key, extent, pieces, -0.22, 0.18)
    return jnp.clip(drawn, -limit, limit).astype(kind)


def setup_inputs(seed: int = 0) -> dict:
    seeds = jax.random.split(jax.random.key(seed), 6)
    queries = draw_queries(jax.random.fold_in(seeds[5], 71), 0)
    keys = bell_draw(seeds[1], (TOKENS, D), 1.0, 6.0, ((0, 32), (1, 16)))
    values = bell_draw(seeds[2], (TOKENS, D), 1.0, 6.0, ((0, 32), (1, 16)))
    gain = jnp.clip(1.0 + 0.15 * jax.random.normal(seeds[3], (D,), jnp.float32), 0.25, 1.75).astype(jnp.bfloat16)
    grad_out = bell_draw(seeds[4], (TOKENS, D), 1.0, 6.0, ((0, 32), (1, 16)))
    return {"queries": queries, "keys": keys, "values": values, "gain": gain, "grad_out": grad_out}


epsilon = 1e-06

def rounded_state(x):
    return lax.optimization_barrier(x.astype(jnp.bfloat16)).astype(jnp.float32)

def reference(queries, keys, values, gain, grad_out):
    count = TOKENS // BLK
    shape = (count, BLK, H, HD)
    q_blocks = queries.reshape(shape)
    k_blocks = keys.reshape(shape)
    v_blocks = values.reshape(shape)
    row_index = jnp.arange(BLK)[:, None]
    col_index = jnp.arange(BLK)[None, :]
    causal = col_index <= row_index

    def masked(left, right):
        scores = jnp.einsum('thd,shd->hts', left.astype(jnp.float32), right.astype(jnp.float32))
        return rounded_state(jnp.where(causal[None], scores, 0.0))

    def forward(running_state, blocks):
        query_block, key_block, value_block = blocks
        weights = masked(query_block, key_block)
        layer_output = jnp.einsum('hts,shd->thd', weights, value_block.astype(jnp.float32))
        layer_output = layer_output + jnp.einsum('nqy,qyx->nqx', query_block.astype(jnp.float32), rounded_state(running_state))
        running_state = running_state + jnp.einsum('unc,unl->ncl', key_block.astype(jnp.float32), value_block.astype(jnp.float32))
        return (running_state, layer_output)
    start = jnp.zeros((H, HD, HD), jnp.float32)
    _, attn = lax.scan(forward, start, (q_blocks, k_blocks, v_blocks))
    attn = attn.reshape(TOKENS, D)
    scaled = grad_out.astype(jnp.float32) * gain.astype(jnp.float32)[None, :]
    inv_rms = lax.rsqrt(lax.optimization_barrier(jnp.mean(attn * attn, axis=-1, keepdims=True)) + epsilon)
    cross = lax.optimization_barrier(jnp.sum(scaled * attn, axis=-1, keepdims=True))
    grad_attn = (scaled * inv_rms - attn * cross * inv_rms ** 3 / D).astype(jnp.bfloat16)
    g_blocks = grad_attn.reshape(shape)

    def query_pass(running_state, blocks):
        key_block, value_block, gradient_block = blocks
        grad_weights = masked(gradient_block, value_block)
        layer_output = jnp.einsum('hts,shk->thk', grad_weights, key_block.astype(jnp.float32))
        layer_output = layer_output + jnp.einsum('acd,cnd->acn', gradient_block.astype(jnp.float32), rounded_state(running_state))
        running_state = running_state + jnp.einsum('unc,unl->ncl', key_block.astype(jnp.float32), value_block.astype(jnp.float32))
        return (running_state, layer_output.astype(jnp.bfloat16))
    _, grad_queries = lax.scan(query_pass, start, (k_blocks, v_blocks, g_blocks))

    def key_pass(running_state, blocks):
        query_block, key_block, value_block, gradient_block = blocks
        weights = masked(query_block, key_block)
        grad_weights = masked(gradient_block, value_block)
        state_halfwidth = rounded_state(running_state)
        key_gradient = jnp.einsum('hts,thk->shk', grad_weights, query_block.astype(jnp.float32))
        key_gradient = key_gradient + jnp.einsum('dft,fbt->dfb', value_block.astype(jnp.float32), state_halfwidth)
        value_gradient = jnp.einsum('hts,thv->shv', weights, gradient_block.astype(jnp.float32))
        value_gradient = value_gradient + jnp.einsum('gjn,jnx->gjx', key_block.astype(jnp.float32), state_halfwidth)
        running_state = running_state + jnp.einsum('fap,fam->apm', query_block.astype(jnp.float32), gradient_block.astype(jnp.float32))
        return (running_state, (key_gradient.astype(jnp.bfloat16), value_gradient.astype(jnp.bfloat16)))
    _, (grad_keys, grad_values) = lax.scan(key_pass, start, (q_blocks, k_blocks, v_blocks, g_blocks), reverse=True)
    return (grad_queries.reshape(TOKENS, D), grad_keys.reshape(TOKENS, D), grad_values.reshape(TOKENS, D))
```

```python
import jax
import jax.numpy as jnp
from jax import lax
from jax.experimental import pallas as pl
from jax.experimental.pallas import tpu as pltpu
from jax.sharding import PartitionSpec as P

HD = 128
D = 4096
BLK = 512
TILE = 256
HEADS = 2
SEQ = 32
TP = 16
EPSILON = 1e-06

F32 = jnp.float32
BF16 = jnp.bfloat16
VMEM = pl.BlockSpec(memory_space=pltpu.VMEM)


def nn(a, b):
    return lax.dot_general(a, b, (((1,), (0,)), ((), ())), preferred_element_type=F32)


def nt(a, b):
    return lax.dot_general(a, b, (((1,), (1,)), ((), ())), preferred_element_type=F32)


def tn(a, b):
    return lax.dot_general(a, b, (((0,), (0,)), ((), ())), preferred_element_type=F32)


def lower():
    row = lax.broadcasted_iota(jnp.int32, (TILE, TILE), 0)
    col = lax.broadcasted_iota(jnp.int32, (TILE, TILE), 1)
    return col <= row


def upper():
    row = lax.broadcasted_iota(jnp.int32, (TILE, TILE), 0)
    col = lax.broadcasted_iota(jnp.int32, (TILE, TILE), 1)
    return col >= row


def call(kernel, outs, scratch=(), flops=0):
    return pl.pallas_call(
        kernel,
        out_shape=outs,
        scratch_shapes=list(scratch),
        compiler_params=pltpu.CompilerParams(vmem_limit_bytes=24 * 2**20),
        cost_estimate=pl.CostEstimate(flops=flops, bytes_accessed=2**20, transcendentals=0),
    )


def state_kernel(left_ref, right_ref, out_ref):
    for h in range(HEADS):
        cols = slice(h * HD, (h + 1) * HD)
        out_ref[cols, :] = tn(left_ref[:, cols], right_ref[:, cols])


def before_kernel(in_ref, out_ref):
    acc = jnp.zeros((8, 128), F32)
    for b in range(SEQ):
        out_ref[b] = acc
        acc = acc + in_ref[b]


def after_kernel(in_ref, out_ref):
    acc = jnp.zeros((8, 128), F32)
    for b in reversed(range(SEQ)):
        out_ref[b] = acc
        acc = acc + in_ref[b]


def forward_kernel(q_ref, k_ref, v_ref, gain_ref, go_ref, state_ref, attn_ref, sums_ref):
    mask = lower()
    square = []
    cross = []
    for t in range(BLK // TILE):
        rows = slice(t * TILE, (t + 1) * TILE)
        sq = jnp.zeros((TILE, HD), F32)
        cr = jnp.zeros((TILE, HD), F32)
        for h in range(HEADS):
            cols = slice(h * HD, (h + 1) * HD)
            q = q_ref[rows, cols]
            attn = nn(q, state_ref[cols, :].astype(BF16))
            for s in range(t + 1):
                srows = slice(s * TILE, (s + 1) * TILE)
                scores = nt(q, k_ref[srows, cols])
                if s == t:
                    scores = jnp.where(mask, scores, 0.0)
                attn = attn + nn(scores.astype(BF16), v_ref[srows, cols])
            attn_ref[rows, cols] = attn
            scaled = go_ref[rows, cols].astype(F32) * gain_ref[:, cols].astype(F32)
            sq = sq + attn * attn
            cr = cr + scaled * attn
        square.append(jnp.sum(sq, axis=1, keepdims=True))
        cross.append(jnp.sum(cr, axis=1, keepdims=True))
    lane = lax.broadcasted_iota(jnp.int32, (BLK, 128), 1)
    both = jnp.where(lane == 0, jnp.concatenate(square, axis=0), jnp.concatenate(cross, axis=0))
    turned = both.T
    for i in range(BLK // 128):
        part = slice(i * 128, (i + 1) * 128)
        sums_ref[:, i, :] = jnp.broadcast_to(turned[0:1, part], (TP, 128))
        sums_ref[:, i + 4, :] = jnp.broadcast_to(turned[1:2, part], (TP, 128))


def middle_kernel(q_ref, k_ref, v_ref, gain_ref, go_ref, state_ref, attn_ref, sums_ref, g_ref, gq_ref, out_ref):
    mask = lower()
    total = jnp.sum(sums_ref[...], axis=0)
    square = jnp.concatenate([total[i : i + 1] for i in range(4)], axis=1)
    cross = jnp.concatenate([total[i : i + 1] for i in range(4, 8)], axis=1)
    inv = lax.rsqrt(square / D + EPSILON)
    factor = cross * (inv * inv * inv) / D
    row = lax.broadcasted_iota(jnp.int32, (128, BLK), 0)
    turned = jnp.where(row == 0, inv, factor).T
    inv = turned[:, 0:1]
    factor = turned[:, 1:2]
    for h in range(HEADS):
        cols = slice(h * HD, (h + 1) * HD)
        scaled = go_ref[:, cols].astype(F32) * gain_ref[:, cols].astype(F32)
        g = (scaled * inv - attn_ref[:, cols] * factor).astype(BF16)
        g_ref[:, cols] = g
        out_ref[cols, :] = tn(q_ref[:, cols], g)
        state = state_ref[cols, :].astype(BF16)
        for t in range(BLK // TILE):
            rows = slice(t * TILE, (t + 1) * TILE)
            gt = g[rows]
            grad = nt(gt, state)
            for s in range(t + 1):
                srows = slice(s * TILE, (s + 1) * TILE)
                scores = nt(gt, v_ref[srows, cols])
                if s == t:
                    scores = jnp.where(mask, scores, 0.0)
                grad = grad + nn(scores.astype(BF16), k_ref[srows, cols])
            gq_ref[rows, cols] = grad.astype(BF16)


def last_kernel(q_ref, k_ref, v_ref, g_ref, state_ref, gk_ref, gv_ref):
    mask = upper()
    for h in range(HEADS):
        cols = slice(h * HD, (h + 1) * HD)
        state = state_ref[cols, :].astype(BF16)
        for s in range(BLK // TILE):
            rows = slice(s * TILE, (s + 1) * TILE)
            k = k_ref[rows, cols]
            v = v_ref[rows, cols]
            gk = nt(v, state)
            gv = nn(k, state)
            for t in range(s, BLK // TILE):
                trows = slice(t * TILE, (t + 1) * TILE)
                q = q_ref[trows, cols]
                g = g_ref[trows, cols]
                scores = nt(k, q)
                grads = nt(v, g)
                if s == t:
                    scores = jnp.where(mask, scores, 0.0)
                    grads = jnp.where(mask, grads, 0.0)
                gk = gk + nn(grads.astype(BF16), q)
                gv = gv + nn(scores.astype(BF16), g)
            gk_ref[rows, cols] = gk.astype(BF16)
            gv_ref[rows, cols] = gv.astype(BF16)


def carried(total, kernel):
    pieces = lax.all_to_all(total.reshape(SEQ, 8, 128), "seq", 0, 0, tiled=True)
    sums = call(kernel, jax.ShapeDtypeStruct((SEQ, 8, 128), F32))(pieces)
    back = lax.all_to_all(sums, "seq", 0, 0, tiled=True)
    return back.reshape(HEADS * HD, HD)


def local(queries, keys, values, gain, grad_out):
    rows, width = queries.shape
    gain = gain.reshape(1, width)
    state_shape = jax.ShapeDtypeStruct((HEADS * HD, HD), F32)
    half = jax.ShapeDtypeStruct((rows, width), BF16)
    key_terms = call(state_kernel, state_shape)(keys, values)
    key_state = carried(key_terms, before_kernel)
    attn, sums = call(
        forward_kernel,
        (jax.ShapeDtypeStruct((rows, width), F32), jax.ShapeDtypeStruct((TP, 8, 128), F32)),
    )(queries, keys, values, gain, grad_out, key_state)
    sums = lax.all_to_all(sums, "tp", 0, 0, tiled=True)
    grad_attn, grad_q, query_terms = call(middle_kernel, (half, half, state_shape))(
        queries, keys, values, gain, grad_out, key_state, attn, sums
    )
    grad_state = carried(query_terms, after_kernel)
    grad_k, grad_v = call(last_kernel, (half, half))(queries, keys, values, grad_attn, grad_state)
    return grad_q, grad_k, grad_v


def solution(mesh):
    placed = (P("seq", "tp"), P("seq", "tp"), P("seq", "tp"), P("tp"), P("seq", "tp"))
    return jax.shard_map(
        local,
        mesh=mesh,
        in_specs=placed,
        out_specs=(P("seq", "tp"), P("seq", "tp"), P("seq", "tp")),
        check_vma=False,
    )
```

```python
import jax
import jax.numpy as jnp
from jax import lax
from jax.experimental import pallas as pl
from jax.experimental.pallas import tpu as pltpu
from jax.sharding import PartitionSpec as P

HD = 128
D = 4096
BLK = 512
TILE = 256
HEADS = 2
WIDTH = HEADS * HD
SEQ = 32
TP = 16
CHUNKS = 4
EPSILON = 1e-06

F32 = jnp.float32
BF16 = jnp.bfloat16


def nn(a, b):
    return lax.dot_general(a, b, (((1,), (0,)), ((), ())), preferred_element_type=F32)


def nt(a, b):
    return lax.dot_general(a, b, (((1,), (1,)), ((), ())), preferred_element_type=F32)


def tn(a, b):
    return lax.dot_general(a, b, (((0,), (0,)), ((), ())), preferred_element_type=F32)


def head(h):
    return slice(h * HD, (h + 1) * HD)


def tile(t):
    return slice(t * TILE, (t + 1) * TILE)


def masks():
    row = lax.broadcasted_iota(jnp.int32, (TILE, TILE), 0)
    col = lax.broadcasted_iota(jnp.int32, (TILE, TILE), 1)
    return col <= row, col >= row


def call(kernel, outs, flops, moved, limit=16, **spec):
    return pl.pallas_call(
        kernel,
        out_shape=outs,
        compiler_params=pltpu.CompilerParams(vmem_limit_bytes=limit * 2**20),
        cost_estimate=pl.CostEstimate(flops=flops, bytes_accessed=moved, transcendentals=0),
        **spec,
    )


def state_kernel(k_hbm, v_hbm, out_ref, k_ref, v_ref, sems):
    copies = []
    for c in range(CHUNKS):
        rows = pl.ds(c * (BLK // CHUNKS), BLK // CHUNKS)
        pair = (
            pltpu.make_async_copy(k_hbm.at[rows], k_ref.at[rows], sems.at[0, c]),
            pltpu.make_async_copy(v_hbm.at[rows], v_ref.at[rows], sems.at[1, c]),
        )
        for copy in pair:
            copy.start()
        copies.append(pair)
    total = [None] * HEADS
    for c in range(CHUNKS):
        for copy in copies[c]:
            copy.wait()
        rows = slice(c * (BLK // CHUNKS), (c + 1) * (BLK // CHUNKS))
        for h in range(HEADS):
            term = tn(v_ref[rows, head(h)], k_ref[rows, head(h)])
            total[h] = term if c == 0 else total[h] + term
    for h in range(HEADS):
        out_ref[head(h), :] = total[h]


def before_kernel(in_ref, out_ref):
    acc = jnp.zeros((8, 128), F32)
    for b in range(SEQ):
        out_ref[b] = acc
        acc = acc + in_ref[b]


def after_kernel(in_ref, out_ref):
    acc = jnp.zeros((8, 128), F32)
    for b in reversed(range(SEQ)):
        out_ref[b] = acc
        acc = acc + in_ref[b]


def local_kernel(q_ref, k_ref, v_ref, gain_ref, go_ref, inner_ref, scaled_ref):
    lower, _ = masks()
    scaled_ref[...] = (go_ref[...].astype(F32) * gain_ref[...].astype(F32)).T
    for h in range(HEADS):
        for t in range(BLK // TILE):
            attn = None
            for s in range(t + 1):
                scores = nt(q_ref[tile(t), head(h)], k_ref[tile(s), head(h)])
                if s == t:
                    scores = jnp.where(lower, scores, 0.0)
                term = nn(scores.astype(BF16), v_ref[tile(s), head(h)])
                attn = term if attn is None else attn + term
            inner_ref[head(h), tile(t)] = attn.T


def attn_kernel(q_ref, inner_ref, scaled_ref, state_ref, attn_ref, sums_ref):
    square = jnp.zeros((8, BLK), F32)
    cross = jnp.zeros((8, BLK), F32)
    for h in range(HEADS):
        attn = inner_ref[head(h), :] + nt(state_ref[head(h), :].astype(BF16), q_ref[:, head(h)])
        attn_ref[head(h), :] = attn
        square = square + jnp.sum((attn * attn).reshape(HD // 8, 8, BLK), axis=0)
        cross = cross + jnp.sum((scaled_ref[head(h), :] * attn).reshape(HD // 8, 8, BLK), axis=0)
    square = jnp.sum(square, axis=0, keepdims=True)
    cross = jnp.sum(cross, axis=0, keepdims=True)
    rows = [x[:, i * 128 : (i + 1) * 128] for x in (square, cross) for i in range(BLK // 128)]
    sums_ref[...] = jnp.broadcast_to(jnp.concatenate(rows, axis=0)[None], (TP, 8, 128))


def grad_kernel(q_ref, scaled_ref, attn_ref, sums_ref, g_ref, out_ref):
    total = jnp.sum(sums_ref[...], axis=0)
    inv = lax.rsqrt(total[0:4] / D + EPSILON)
    factor = total[4:8] * (inv * inv * inv) / D
    inv = jnp.concatenate([inv[i : i + 1] for i in range(BLK // 128)], axis=1)
    factor = jnp.concatenate([factor[i : i + 1] for i in range(BLK // 128)], axis=1)
    for h in range(HEADS):
        g = (scaled_ref[head(h), :] * inv - attn_ref[head(h), :] * factor).astype(BF16)
        g_ref[head(h), :] = g
        out_ref[head(h), :] = nn(g, q_ref[:, head(h)])


def inner_kernel(q_ref, k_ref, v_ref, g_ref, state_ref, gq_ref, gk_ref, gv_ref):
    lower, upper = masks()
    for h in range(HEADS):
        g = g_ref[head(h), :].T
        state = state_ref[head(h), :].astype(BF16)
        for t in range(BLK // TILE):
            grad = nn(g[tile(t)], state)
            for s in range(t + 1):
                scores = nt(g[tile(t)], v_ref[tile(s), head(h)])
                if s == t:
                    scores = jnp.where(lower, scores, 0.0)
                grad = grad + nn(scores.astype(BF16), k_ref[tile(s), head(h)])
            gq_ref[tile(t), head(h)] = grad.astype(BF16)
        for s in range(BLK // TILE):
            gk = gv = None
            for t in range(s, BLK // TILE):
                q = q_ref[tile(t), head(h)]
                scores = nt(k_ref[tile(s), head(h)], q)
                grads = nn(v_ref[tile(s), head(h)], g_ref[head(h), tile(t)])
                if s == t:
                    scores = jnp.where(upper, scores, 0.0)
                    grads = jnp.where(upper, grads, 0.0)
                gk_term = nn(grads.astype(BF16), q)
                gv_term = nn(scores.astype(BF16), g[tile(t)])
                gk = gk_term if gk is None else gk + gk_term
                gv = gv_term if gv is None else gv + gv_term
            gk_ref[tile(s), head(h)] = gk
            gv_ref[tile(s), head(h)] = gv


def last_kernel(k_ref, v_ref, gk_in_ref, gv_in_ref, state_ref, gk_ref, gv_ref):
    for h in range(HEADS):
        state = state_ref[head(h), :].astype(BF16)
        gk_ref[:, head(h)] = (gk_in_ref[:, head(h)] + nn(v_ref[:, head(h)], state)).astype(BF16)
        gv_ref[:, head(h)] = (gv_in_ref[:, head(h)] + nt(k_ref[:, head(h)], state)).astype(BF16)


def carried(total, kernel):
    pieces = lax.all_to_all(total.reshape(SEQ, 8, 128), "seq", 0, 0, tiled=True)
    sums = call(kernel, jax.ShapeDtypeStruct((SEQ, 8, 128), F32), 2**15, 2**18)(pieces)
    back = lax.all_to_all(sums, "seq", 0, 0, tiled=True)
    return back.reshape(WIDTH, HD)


def local(queries, keys, values, gain, grad_out):
    gain = gain.reshape(1, WIDTH)
    state_shape = jax.ShapeDtypeStruct((WIDTH, HD), F32)
    half = jax.ShapeDtypeStruct((BLK, WIDTH), BF16)
    full = jax.ShapeDtypeStruct((BLK, WIDTH), F32)
    half_turned = jax.ShapeDtypeStruct((WIDTH, BLK), BF16)
    full_turned = jax.ShapeDtypeStruct((WIDTH, BLK), F32)
    small = 2 * HEADS * BLK * HD * HD
    square = 2 * HEADS * BLK * BLK * HD
    key_terms = call(
        state_kernel,
        state_shape,
        small,
        2**19,
        limit=60,
        in_specs=[pl.BlockSpec(memory_space=pltpu.HBM)] * 2,
        scratch_shapes=[
            pltpu.VMEM((BLK, WIDTH), BF16),
            pltpu.VMEM((BLK, WIDTH), BF16),
            pltpu.SemaphoreType.DMA((2, CHUNKS)),
        ],
    )(keys, values)
    key_state = carried(key_terms, before_kernel)
    inner, scaled = call(local_kernel, (full_turned, full_turned), 2 * square, 2**21)(
        queries, keys, values, gain, grad_out
    )
    attn, sums = call(
        attn_kernel, (full_turned, jax.ShapeDtypeStruct((TP, 8, 128), F32)), small, 2**21
    )(queries, inner, scaled, key_state)
    sums = lax.all_to_all(sums, "tp", 0, 0, tiled=True)
    grad_attn, query_terms = call(grad_kernel, (half_turned, state_shape), small, 2**21)(
        queries, scaled, attn, sums
    )
    grad_state = carried(query_terms, after_kernel)
    grad_q, inner_k, inner_v = call(inner_kernel, (half, full, full), 6 * square, 2**22)(
        queries, keys, values, grad_attn, key_state
    )
    grad_k, grad_v = call(last_kernel, (half, half), 2 * small, 2**21)(
        keys, values, inner_k, inner_v, grad_state
    )
    return grad_q, grad_k, grad_v


def solution(mesh):
    placed = (P("seq", "tp"), P("seq", "tp"), P("seq", "tp"), P("tp"), P("seq", "tp"))
    return jax.shard_map(
        local,
        mesh=mesh,
        in_specs=placed,
        out_specs=(P("seq", "tp"), P("seq", "tp"), P("seq", "tp")),
        check_vma=False,
    )
```

```python
import jax
import jax.numpy as jnp
from jax import lax
from jax.experimental import pallas as pl
from jax.experimental.pallas import tpu as pltpu
from jax.sharding import PartitionSpec as P

HD = 128
D = 4096
BLK = 512
TILE = 256
HEADS = 2
WIDTH = HEADS * HD
SEQ = 32
TP = 16
EPSILON = 1e-06

F32 = jnp.float32
BF16 = jnp.bfloat16


def nn(a, b):
    return lax.dot_general(a, b, (((1,), (0,)), ((), ())), preferred_element_type=F32)


def nt(a, b):
    return lax.dot_general(a, b, (((1,), (1,)), ((), ())), preferred_element_type=F32)


def tn(a, b):
    return lax.dot_general(a, b, (((0,), (0,)), ((), ())), preferred_element_type=F32)


def head(h):
    return slice(h * HD, (h + 1) * HD)


def tile(t):
    return slice(t * TILE, (t + 1) * TILE)


def masks():
    row = lax.broadcasted_iota(jnp.int32, (TILE, TILE), 0)
    col = lax.broadcasted_iota(jnp.int32, (TILE, TILE), 1)
    return col <= row, col >= row


def call(kernel, outs, flops, moved, limit=16, **spec):
    return pl.pallas_call(
        kernel,
        out_shape=outs,
        compiler_params=pltpu.CompilerParams(vmem_limit_bytes=limit * 2**20),
        cost_estimate=pl.CostEstimate(flops=flops, bytes_accessed=moved, transcendentals=0),
        **spec,
    )


def state_kernel(k_hbm, v_hbm, out_ref, k_ref, v_ref, sems):
    copies = (
        pltpu.make_async_copy(k_hbm, k_ref, sems.at[0]),
        pltpu.make_async_copy(v_hbm, v_ref, sems.at[1]),
    )
    for copy in copies:
        copy.start()
    for copy in copies:
        copy.wait()
    for h in range(HEADS):
        out_ref[head(h), :] = tn(v_ref[:, head(h)], k_ref[:, head(h)])


def before_kernel(in_ref, out_ref):
    acc = jnp.zeros((8, 128), F32)
    for b in range(SEQ):
        out_ref[b] = acc
        acc = acc + in_ref[b]


def after_kernel(in_ref, out_ref):
    acc = jnp.zeros((8, 128), F32)
    for b in reversed(range(SEQ)):
        out_ref[b] = acc
        acc = acc + in_ref[b]


def local_kernel(q_ref, k_ref, v_ref, gain_ref, go_ref, inner_ref, scaled_ref):
    lower, _ = masks()
    scaled_ref[...] = (go_ref[...].astype(F32) * gain_ref[...].astype(F32)).T
    for h in range(HEADS):
        for t in range(BLK // TILE):
            attn = None
            for s in range(t + 1):
                scores = nt(q_ref[tile(t), head(h)], k_ref[tile(s), head(h)])
                if s == t:
                    scores = jnp.where(lower, scores, 0.0)
                term = nn(scores.astype(BF16), v_ref[tile(s), head(h)])
                attn = term if attn is None else attn + term
            inner_ref[head(h), tile(t)] = attn.T


def attn_kernel(q_ref, inner_ref, scaled_ref, state_ref, attn_ref, sums_ref):
    square = jnp.zeros((8, BLK), F32)
    cross = jnp.zeros((8, BLK), F32)
    for h in range(HEADS):
        attn = inner_ref[head(h), :] + nt(state_ref[head(h), :].astype(BF16), q_ref[:, head(h)])
        attn_ref[head(h), :] = attn
        square = square + jnp.sum((attn * attn).reshape(HD // 8, 8, BLK), axis=0)
        cross = cross + jnp.sum((scaled_ref[head(h), :] * attn).reshape(HD // 8, 8, BLK), axis=0)
    square = jnp.sum(square, axis=0, keepdims=True)
    cross = jnp.sum(cross, axis=0, keepdims=True)
    rows = [x[:, i * 128 : (i + 1) * 128] for x in (square, cross) for i in range(BLK // 128)]
    sums_ref[...] = jnp.broadcast_to(jnp.concatenate(rows, axis=0)[None], (TP, 8, 128))


def grad_kernel(q_ref, scaled_ref, attn_ref, sums_ref, g_ref, out_ref):
    total = jnp.sum(sums_ref[...], axis=0)
    inv = lax.rsqrt(total[0:4] / D + EPSILON)
    factor = total[4:8] * (inv * inv * inv) / D
    inv = jnp.concatenate([inv[i : i + 1] for i in range(BLK // 128)], axis=1)
    factor = jnp.concatenate([factor[i : i + 1] for i in range(BLK // 128)], axis=1)
    for h in range(HEADS):
        g = (scaled_ref[head(h), :] * inv - attn_ref[head(h), :] * factor).astype(BF16)
        g_ref[head(h), :] = g
        out_ref[head(h), :] = nn(g, q_ref[:, head(h)])


def inner_kernel(q_ref, k_ref, v_ref, g_ref, state_ref, gq_ref, gk_ref, gv_ref):
    lower, upper = masks()
    for h in range(HEADS):
        g = g_ref[head(h), :].T
        state = state_ref[head(h), :].astype(BF16)
        for t in range(BLK // TILE):
            grad = nn(g[tile(t)], state)
            for s in range(t + 1):
                scores = nt(g[tile(t)], v_ref[tile(s), head(h)])
                if s == t:
                    scores = jnp.where(lower, scores, 0.0)
                grad = grad + nn(scores.astype(BF16), k_ref[tile(s), head(h)])
            gq_ref[tile(t), head(h)] = grad.astype(BF16)
        for s in range(BLK // TILE):
            gk = gv = None
            for t in range(s, BLK // TILE):
                q = q_ref[tile(t), head(h)]
                scores = nt(k_ref[tile(s), head(h)], q)
                grads = nn(v_ref[tile(s), head(h)], g_ref[head(h), tile(t)])
                if s == t:
                    scores = jnp.where(upper, scores, 0.0)
                    grads = jnp.where(upper, grads, 0.0)
                gk_term = nn(grads.astype(BF16), q)
                gv_term = nn(scores.astype(BF16), g[tile(t)])
                gk = gk_term if gk is None else gk + gk_term
                gv = gv_term if gv is None else gv + gv_term
            gk_ref[tile(s), head(h)] = gk
            gv_ref[tile(s), head(h)] = gv


def last_kernel(k_ref, v_ref, gk_in_ref, gv_in_ref, state_ref, gk_hbm, gv_hbm, gk_ref, gv_ref, sems):
    state = [state_ref[head(h), :].astype(BF16) for h in range(HEADS)]
    copies = []
    for t in range(BLK // TILE):
        for h in range(HEADS):
            gk = gk_in_ref[tile(t), head(h)] + nn(v_ref[tile(t), head(h)], state[h])
            gk_ref[tile(t), head(h)] = gk.astype(BF16)
            gv = gv_in_ref[tile(t), head(h)] + nt(k_ref[tile(t), head(h)], state[h])
            gv_ref[tile(t), head(h)] = gv.astype(BF16)
        for i, (mine, out) in enumerate(((gk_ref, gk_hbm), (gv_ref, gv_hbm))):
            copies.append(pltpu.make_async_copy(mine.at[tile(t)], out.at[tile(t)], sems.at[i, t]))
            copies[-1].start()
    for copy in copies:
        copy.wait()


def carried(total, kernel):
    pieces = lax.all_to_all(total.reshape(SEQ, 8, 128), "seq", 0, 0, tiled=True)
    sums = call(kernel, pltpu.VMEM((SEQ, 8, 128), F32), 2**15, 2**18)(pieces)
    back = lax.all_to_all(sums, "seq", 0, 0, tiled=True)
    return back.reshape(WIDTH, HD)


def local(queries, keys, values, gain, grad_out):
    gain = gain.reshape(1, WIDTH)
    state_shape = pltpu.VMEM((WIDTH, HD), F32)
    half = jax.ShapeDtypeStruct((BLK, WIDTH), BF16)
    full = jax.ShapeDtypeStruct((BLK, WIDTH), F32)
    half_turned = jax.ShapeDtypeStruct((WIDTH, BLK), BF16)
    full_turned = jax.ShapeDtypeStruct((WIDTH, BLK), F32)
    small = 2 * HEADS * BLK * HD * HD
    square = 2 * HEADS * BLK * BLK * HD
    key_terms = call(
        state_kernel,
        state_shape,
        small,
        2**19,
        in_specs=[pl.BlockSpec(memory_space=pltpu.HBM)] * 2,
        scratch_shapes=[
            pltpu.VMEM((BLK, WIDTH), BF16),
            pltpu.VMEM((BLK, WIDTH), BF16),
            pltpu.SemaphoreType.DMA((2,)),
        ],
    )(pltpu.with_memory_space_constraint(keys, pltpu.HBM), pltpu.with_memory_space_constraint(values, pltpu.HBM))
    key_state = carried(key_terms, before_kernel)
    inner, scaled = call(local_kernel, (full_turned, full_turned), 2 * square, 2**21)(
        queries, keys, values, gain, grad_out
    )
    attn, sums = call(
        attn_kernel, (full_turned, jax.ShapeDtypeStruct((TP, 8, 128), F32)), small, 2**21
    )(queries, inner, scaled, key_state)
    sums = lax.all_to_all(sums, "tp", 0, 0, tiled=True)
    grad_attn, query_terms = call(grad_kernel, (half_turned, state_shape), small, 2**21)(
        queries, scaled, attn, sums
    )
    grad_state = carried(query_terms, after_kernel)
    grad_q, inner_k, inner_v = call(inner_kernel, (half, full, full), 6 * square, 2**22)(
        queries, keys, values, grad_attn, key_state
    )
    grad_k, grad_v = call(
        last_kernel,
        (half, half),
        2 * small,
        2**21,
        in_specs=[pl.BlockSpec(memory_space=pltpu.VMEM)] * 5,
        out_specs=(pl.BlockSpec(memory_space=pltpu.HBM),) * 2,
        scratch_shapes=[
            pltpu.VMEM((BLK, WIDTH), BF16),
            pltpu.VMEM((BLK, WIDTH), BF16),
            pltpu.SemaphoreType.DMA((2, BLK // TILE)),
        ],
    )(keys, values, inner_k, inner_v, grad_state)
    return grad_q, grad_k, grad_v


def solution(mesh):
    placed = (P("seq", "tp"), P("seq", "tp"), P("seq", "tp"), P("tp"), P("seq", "tp"))
    return jax.shard_map(
        local,
        mesh=mesh,
        in_specs=placed,
        out_specs=(P("seq", "tp"), P("seq", "tp"), P("seq", "tp")),
        check_vma=False,
    )
```

```python
import functools

import jax
import jax.numpy as jnp
from jax import lax
from jax.experimental import pallas as pl
from jax.experimental.pallas import tpu as pltpu
from jax.sharding import PartitionSpec as P

HD = 128
D = 4096
BLK = 512
TILE = 256
HEADS = 2
WIDTH = HEADS * HD
SEQ = 32
TP = 16
EPSILON = 1e-06
FIRST_BEFORE = 5 * 4 + 2
FIRST_AFTER = 4 * 4 + 2
FIRST_TP = 4 * 2 + 1

F32 = jnp.float32
BF16 = jnp.bfloat16


def nn(a, b):
    return lax.dot_general(a, b, (((1,), (0,)), ((), ())), preferred_element_type=F32)


def nt(a, b):
    return lax.dot_general(a, b, (((1,), (1,)), ((), ())), preferred_element_type=F32)


def tn(a, b):
    return lax.dot_general(a, b, (((0,), (0,)), ((), ())), preferred_element_type=F32)


def head(h):
    return slice(h * HD, (h + 1) * HD)


def tile(t):
    return slice(t * TILE, (t + 1) * TILE)


def masks():
    row = lax.broadcasted_iota(jnp.int32, (TILE, TILE), 0)
    col = lax.broadcasted_iota(jnp.int32, (TILE, TILE), 1)
    return col <= row, col >= row


def call(kernel, outs, flops, moved, limit=16, **spec):
    return pl.pallas_call(
        kernel,
        out_shape=outs,
        compiler_params=pltpu.CompilerParams(vmem_limit_bytes=limit * 2**20),
        cost_estimate=pl.CostEstimate(flops=flops, bytes_accessed=moved, transcendentals=0),
        **spec,
    )


def state_kernel(k_hbm, v_hbm, gain_hbm, out_ref, gain_ref, k_ref, v_ref, sems):
    copies = (
        pltpu.make_async_copy(k_hbm, k_ref, sems.at[0]),
        pltpu.make_async_copy(v_hbm, v_ref, sems.at[1]),
        pltpu.make_async_copy(gain_hbm, gain_ref, sems.at[2]),
    )
    for copy in copies:
        copy.start()
    for copy in copies:
        copy.wait()
    for h in range(HEADS):
        out_ref[head(h), :] = tn(v_ref[:, head(h)], k_ref[:, head(h)])


def slot(block, first):
    return (block - first) % SEQ


def before_kernel(first, in_ref, out_ref):
    acc = jnp.zeros((8, 128), F32)
    for b in range(SEQ):
        out_ref[slot(b, first)] = acc
        acc = acc + in_ref[slot(b, first)]


def after_kernel(first, in_ref, out_ref):
    acc = jnp.zeros((8, 128), F32)
    for b in reversed(range(SEQ)):
        out_ref[slot(b, first)] = acc
        acc = acc + in_ref[slot(b, first)]


def attn_kernel(q_ref, k_ref, v_ref, gain_ref, go_ref, state_ref, attn_ref, scaled_ref, sums_ref):
    _, upper = masks()
    gain = jnp.broadcast_to(gain_ref[...].astype(F32)[None, :], (8, WIDTH)).T[:, 0:1]
    square = [jnp.zeros((8, TILE), F32) for _ in range(BLK // TILE)]
    cross = [jnp.zeros((8, TILE), F32) for _ in range(BLK // TILE)]
    for h in range(HEADS):
        state = state_ref[head(h), :].astype(BF16)
        v = v_ref[:, head(h)].T
        scaled_ref[head(h), :] = go_ref[:, head(h)].T.astype(F32) * gain[head(h)]
        for t in range(BLK // TILE):
            q = q_ref[tile(t), head(h)]
            attn = nt(state, q)
            for s in range(t + 1):
                scores = nt(k_ref[tile(s), head(h)], q)
                if s == t:
                    scores = jnp.where(upper, scores, 0.0)
                attn = attn + nn(v[:, tile(s)], scores.astype(BF16))
            attn_ref[head(h), tile(t)] = attn
            scaled = scaled_ref[head(h), tile(t)]
            square[t] = square[t] + jnp.sum((attn * attn).reshape(HD // 8, 8, TILE), axis=0)
            cross[t] = cross[t] + jnp.sum((scaled * attn).reshape(HD // 8, 8, TILE), axis=0)
    rows = []
    for kind in (square, cross):
        for part in kind:
            row = jnp.sum(part, axis=0, keepdims=True)
            rows += [row[:, i * 128 : (i + 1) * 128] for i in range(TILE // 128)]
    sums_ref[...] = jnp.broadcast_to(jnp.concatenate(rows, axis=0)[None], (TP, 8, 128))


def grad_kernel(q_ref, scaled_ref, attn_ref, sums_ref, g_ref, out_ref):
    total = jnp.sum(sums_ref[...], axis=0)
    inv = lax.rsqrt(total[0:4] / D + EPSILON)
    factor = total[4:8] * (inv * inv * inv) / D
    inv = jnp.concatenate([inv[i : i + 1] for i in range(BLK // 128)], axis=1)
    factor = jnp.concatenate([factor[i : i + 1] for i in range(BLK // 128)], axis=1)
    for h in range(HEADS):
        g = (scaled_ref[head(h), :] * inv - attn_ref[head(h), :] * factor).astype(BF16)
        g_ref[head(h), :] = g
        out_ref[head(h), :] = nn(g, q_ref[:, head(h)])


def inner_kernel(q_ref, k_ref, v_ref, g_ref, state_ref, gq_ref, gk_ref, gv_ref):
    lower, upper = masks()
    for h in range(HEADS):
        g = g_ref[head(h), :].T
        state = state_ref[head(h), :].astype(BF16)
        for t in range(BLK // TILE):
            grad = nn(g[tile(t)], state)
            for s in range(t + 1):
                scores = nt(g[tile(t)], v_ref[tile(s), head(h)])
                if s == t:
                    scores = jnp.where(lower, scores, 0.0)
                grad = grad + nn(scores.astype(BF16), k_ref[tile(s), head(h)])
            gq_ref[tile(t), head(h)] = grad.astype(BF16)
        for s in range(BLK // TILE):
            gk = gv = None
            for t in range(s, BLK // TILE):
                q = q_ref[tile(t), head(h)]
                scores = nt(k_ref[tile(s), head(h)], q)
                grads = nn(v_ref[tile(s), head(h)], g_ref[head(h), tile(t)])
                if s == t:
                    scores = jnp.where(upper, scores, 0.0)
                    grads = jnp.where(upper, grads, 0.0)
                gk_term = nn(grads.astype(BF16), q)
                gv_term = nn(scores.astype(BF16), g[tile(t)])
                gk = gk_term if gk is None else gk + gk_term
                gv = gv_term if gv is None else gv + gv_term
            gk_ref[tile(s), head(h)] = gk
            gv_ref[tile(s), head(h)] = gv


def last_kernel(k_ref, v_ref, gk_in_ref, gv_in_ref, state_ref, gk_hbm, gv_hbm, gk_ref, gv_ref, sems):
    state = [state_ref[head(h), :].astype(BF16) for h in range(HEADS)]
    copies = []
    for t in range(BLK // TILE):
        for h in range(HEADS):
            gk = gk_in_ref[tile(t), head(h)] + nn(v_ref[tile(t), head(h)], state[h])
            gk_ref[tile(t), head(h)] = gk.astype(BF16)
            gv = gv_in_ref[tile(t), head(h)] + nt(k_ref[tile(t), head(h)], state[h])
            gv_ref[tile(t), head(h)] = gv.astype(BF16)
        for i, (mine, out) in enumerate(((gk_ref, gk_hbm), (gv_ref, gv_hbm))):
            copies.append(pltpu.make_async_copy(mine.at[tile(t)], out.at[tile(t)], sems.at[i, t]))
            copies[-1].start()
    for copy in copies:
        copy.wait()


def listed(size, first):
    return [[(first + i) % size for i in range(size)]]


def carried(total, kernel, first):
    groups = listed(SEQ, first)
    pieces = lax.all_to_all(
        total.reshape(SEQ, 8, 128), "seq", 0, 0, tiled=True, axis_index_groups=groups
    )
    sums = call(
        functools.partial(kernel, first), pltpu.VMEM((SEQ, 8, 128), F32), 2**15, 2**18
    )(pieces)
    back = lax.all_to_all(sums, "seq", 0, 0, tiled=True, axis_index_groups=groups)
    return back.reshape(WIDTH, HD)


def local(queries, keys, values, gain, grad_out):
    state_shape = pltpu.VMEM((WIDTH, HD), F32)
    half = jax.ShapeDtypeStruct((BLK, WIDTH), BF16)
    full = jax.ShapeDtypeStruct((BLK, WIDTH), F32)
    half_turned = jax.ShapeDtypeStruct((WIDTH, BLK), BF16)
    full_turned = jax.ShapeDtypeStruct((WIDTH, BLK), F32)
    small = 2 * HEADS * BLK * HD * HD
    square = 2 * HEADS * BLK * BLK * HD
    keys_here, values_here, gain_here = (
        pltpu.with_memory_space_constraint(x, pltpu.HBM) for x in (keys, values, gain)
    )
    key_terms, gain = call(
        state_kernel,
        (state_shape, pltpu.VMEM((WIDTH,), BF16)),
        small,
        2**19,
        in_specs=[pl.BlockSpec(memory_space=pltpu.HBM)] * 3,
        scratch_shapes=[
            pltpu.VMEM((BLK, WIDTH), BF16),
            pltpu.VMEM((BLK, WIDTH), BF16),
            pltpu.SemaphoreType.DMA((3,)),
        ],
    )(keys_here, values_here, gain_here)
    key_state = carried(key_terms, before_kernel, FIRST_BEFORE)
    attn, scaled, sums = call(
        attn_kernel,
        (full_turned, full_turned, jax.ShapeDtypeStruct((TP, 8, 128), F32)),
        small + 2 * square,
        2**21,
    )(queries, keys, values, gain, grad_out, key_state)
    sums = lax.all_to_all(
        sums, "tp", 0, 0, tiled=True, axis_index_groups=listed(TP, FIRST_TP)
    )
    grad_attn, query_terms = call(grad_kernel, (half_turned, state_shape), small, 2**21)(
        queries, scaled, attn, sums
    )
    grad_state = carried(query_terms, after_kernel, FIRST_AFTER)
    grad_q, inner_k, inner_v = call(inner_kernel, (half, full, full), 6 * square, 2**22)(
        queries, keys, values, grad_attn, key_state
    )
    grad_k, grad_v = call(
        last_kernel,
        (half, half),
        2 * small,
        2**21,
        in_specs=[pl.BlockSpec(memory_space=pltpu.VMEM)] * 5,
        out_specs=(pl.BlockSpec(memory_space=pltpu.HBM),) * 2,
        scratch_shapes=[
            pltpu.VMEM((BLK, WIDTH), BF16),
            pltpu.VMEM((BLK, WIDTH), BF16),
            pltpu.SemaphoreType.DMA((2, BLK // TILE)),
        ],
    )(keys, values, inner_k, inner_v, grad_state)
    return grad_q, grad_k, grad_v


def solution(mesh):
    placed = (P("seq", "tp"), P("seq", "tp"), P("seq", "tp"), P("tp"), P("seq", "tp"))
    return jax.shard_map(
        local,
        mesh=mesh,
        in_specs=placed,
        out_specs=(P("seq", "tp"), P("seq", "tp"), P("seq", "tp")),
        check_vma=False,
    )
```

```python
import jax
import jax.numpy as jnp
from jax import lax
from jax.experimental import pallas as pl
from jax.experimental.pallas import tpu as pltpu
from jax.sharding import PartitionSpec as P

HD = 128
D = 4096
BLK = 512
TILE = 256
HEADS = 2
WIDTH = HEADS * HD
SEQ = 32
HALF = 16
PIECE = 16
TP = 16
EPSILON = 1e-06
Z_A = 0
Z_D = 0
FIRST_A = 6
FIRST_B = 22
FIRST_TP = 9
FIRST_C = 22
FIRST_D = 10

F32 = jnp.float32
BF16 = jnp.bfloat16


def nn(a, b):
    return lax.dot_general(a, b, (((1,), (0,)), ((), ())), preferred_element_type=F32)


def nt(a, b):
    return lax.dot_general(a, b, (((1,), (1,)), ((), ())), preferred_element_type=F32)


def tn(a, b):
    return lax.dot_general(a, b, (((0,), (0,)), ((), ())), preferred_element_type=F32)


def head(h):
    return slice(h * HD, (h + 1) * HD)


def tile(t):
    return slice(t * TILE, (t + 1) * TILE)


def masks():
    row = lax.broadcasted_iota(jnp.int32, (TILE, TILE), 0)
    col = lax.broadcasted_iota(jnp.int32, (TILE, TILE), 1)
    return col <= row, col >= row


def call(kernel, outs, flops, moved, limit=16, **spec):
    return pl.pallas_call(
        kernel,
        out_shape=outs,
        compiler_params=pltpu.CompilerParams(vmem_limit_bytes=limit * 2**20),
        cost_estimate=pl.CostEstimate(flops=flops, bytes_accessed=moved, transcendentals=0),
        **spec,
    )


def listed(size, first):
    return [(first + i) % size for i in range(size)]


def halves(z, first):
    return [[(4 * z + half + i) % SEQ for i in listed(HALF, first)] for half in (0, HALF)]


OWNERS_BEFORE = halves(Z_A, FIRST_A)
BACK_BEFORE = listed(SEQ, FIRST_B)
OUT_AFTER = listed(SEQ, FIRST_C)
OWNERS_AFTER = halves(Z_D, FIRST_D)


def state_kernel(k_hbm, v_hbm, gain_hbm, out_ref, gain_ref, k_ref, v_ref, sems):
    copies = (
        pltpu.make_async_copy(k_hbm, k_ref, sems.at[0]),
        pltpu.make_async_copy(v_hbm, v_ref, sems.at[1]),
        pltpu.make_async_copy(gain_hbm, gain_ref, sems.at[2]),
    )
    for copy in copies:
        copy.start()
    for copy in copies:
        copy.wait()
    for h in range(HEADS):
        out_ref[head(h), :] = tn(v_ref[:, head(h)], k_ref[:, head(h)])


def in_half(z, half):
    place = lax.rem(lax.axis_index("seq") + (SEQ - 4 * z), SEQ)
    return place < HALF if half == 0 else place >= HALF


def before_kernel(in_ref, out_ref):
    for half, owners in enumerate(OWNERS_BEFORE):

        @pl.when(in_half(Z_A, half))
        def _():
            acc = jnp.zeros((PIECE, 128), F32)
            for b in range(SEQ):
                out_ref[BACK_BEFORE.index(b)] = acc
                if b in owners:
                    acc = acc + in_ref[owners.index(b)]


def after_kernel(in_ref, out_ref):
    for half, owners in enumerate(OWNERS_AFTER):

        @pl.when(in_half(Z_D, half))
        def _():
            acc = jnp.zeros((PIECE, 128), F32)
            for b in reversed(range(SEQ)):
                if b in owners:
                    out_ref[owners.index(b)] = acc
                acc = acc + in_ref[OUT_AFTER.index(b)]


def attn_kernel(q_ref, k_ref, v_ref, gain_ref, go_ref, parts_ref, attn_ref, scaled_ref, sums_ref, state_ref):
    for i, pair in enumerate(zip(*OWNERS_BEFORE)):
        part = sum(parts_ref[BACK_BEFORE.index(owner)] for owner in pair)
        state_ref[i * PIECE : (i + 1) * PIECE, :] = part.astype(BF16)
    _, upper = masks()
    gain = jnp.broadcast_to(gain_ref[...].astype(F32)[None, :], (8, WIDTH)).T[:, 0:1]
    square = [jnp.zeros((8, TILE), F32) for _ in range(BLK // TILE)]
    cross = [jnp.zeros((8, TILE), F32) for _ in range(BLK // TILE)]
    for h in range(HEADS):
        state = state_ref[head(h), :]
        v = v_ref[:, head(h)].T
        scaled_ref[head(h), :] = go_ref[:, head(h)].T.astype(F32) * gain[head(h)]
        for t in range(BLK // TILE):
            q = q_ref[tile(t), head(h)]
            attn = nt(state, q)
            for s in range(t + 1):
                scores = nt(k_ref[tile(s), head(h)], q)
                if s == t:
                    scores = jnp.where(upper, scores, 0.0)
                attn = attn + nn(v[:, tile(s)], scores.astype(BF16))
            attn_ref[head(h), tile(t)] = attn
            scaled = scaled_ref[head(h), tile(t)]
            square[t] = square[t] + jnp.sum((attn * attn).reshape(HD // 8, 8, TILE), axis=0)
            cross[t] = cross[t] + jnp.sum((scaled * attn).reshape(HD // 8, 8, TILE), axis=0)
    rows = []
    for kind in (square, cross):
        for part in kind:
            row = jnp.sum(part, axis=0, keepdims=True)
            rows += [row[:, i * 128 : (i + 1) * 128] for i in range(TILE // 128)]
    sums_ref[...] = jnp.broadcast_to(jnp.concatenate(rows, axis=0)[None], (TP, 8, 128))


def grad_kernel(q_ref, scaled_ref, attn_ref, sums_ref, g_ref, out_ref):
    total = jnp.sum(sums_ref[...], axis=0)
    inv = lax.rsqrt(total[0:4] / D + EPSILON)
    factor = total[4:8] * (inv * inv * inv) / D
    inv = jnp.concatenate([inv[i : i + 1] for i in range(BLK // 128)], axis=1)
    factor = jnp.concatenate([factor[i : i + 1] for i in range(BLK // 128)], axis=1)
    for h in range(HEADS):
        g = (scaled_ref[head(h), :] * inv - attn_ref[head(h), :] * factor).astype(BF16)
        g_ref[head(h), :] = g
        terms = nn(g, q_ref[:, head(h)])
        for i in range(HD // PIECE):
            part = terms[i * PIECE : (i + 1) * PIECE]
            for owners in OWNERS_AFTER:
                out_ref[OUT_AFTER.index(owners[h * (HD // PIECE) + i])] = part


def inner_kernel(q_ref, k_ref, v_ref, g_ref, state_ref, gq_ref, gk_ref, gv_ref):
    lower, upper = masks()
    for h in range(HEADS):
        g = g_ref[head(h), :].T
        state = state_ref[head(h), :]
        for t in range(BLK // TILE):
            grad = nn(g[tile(t)], state)
            for s in range(t + 1):
                scores = nt(g[tile(t)], v_ref[tile(s), head(h)])
                if s == t:
                    scores = jnp.where(lower, scores, 0.0)
                grad = grad + nn(scores.astype(BF16), k_ref[tile(s), head(h)])
            gq_ref[tile(t), head(h)] = grad.astype(BF16)
        for s in range(BLK // TILE):
            gk = gv = None
            for t in range(s, BLK // TILE):
                q = q_ref[tile(t), head(h)]
                scores = nt(k_ref[tile(s), head(h)], q)
                grads = nn(v_ref[tile(s), head(h)], g_ref[head(h), tile(t)])
                if s == t:
                    scores = jnp.where(upper, scores, 0.0)
                    grads = jnp.where(upper, grads, 0.0)
                gk_term = nn(grads.astype(BF16), q)
                gv_term = nn(scores.astype(BF16), g[tile(t)])
                gk = gk_term if gk is None else gk + gk_term
                gv = gv_term if gv is None else gv + gv_term
            gk_ref[tile(s), head(h)] = gk
            gv_ref[tile(s), head(h)] = gv


def last_kernel(k_ref, v_ref, gk_in_ref, gv_in_ref, state_ref, gk_hbm, gv_hbm, gk_ref, gv_ref, sems):
    state = [state_ref[head(h), :].astype(BF16) for h in range(HEADS)]
    copies = []
    for t in range(BLK // TILE):
        for h in range(HEADS):
            gk = gk_in_ref[tile(t), head(h)] + nn(v_ref[tile(t), head(h)], state[h])
            gk_ref[tile(t), head(h)] = gk.astype(BF16)
            gv = gv_in_ref[tile(t), head(h)] + nt(k_ref[tile(t), head(h)], state[h])
            gv_ref[tile(t), head(h)] = gv.astype(BF16)
        for i, (mine, out) in enumerate(((gk_ref, gk_hbm), (gv_ref, gv_hbm))):
            copies.append(pltpu.make_async_copy(mine.at[tile(t)], out.at[tile(t)], sems.at[i, t]))
            copies[-1].start()
    for copy in copies:
        copy.wait()


def exchange(pieces, axis, groups):
    return lax.all_to_all(pieces, axis, 0, 0, tiled=True, axis_index_groups=groups)


def local(queries, keys, values, gain, grad_out):
    state_shape = pltpu.VMEM((WIDTH, HD), F32)
    half = jax.ShapeDtypeStruct((BLK, WIDTH), BF16)
    full = jax.ShapeDtypeStruct((BLK, WIDTH), F32)
    half_turned = jax.ShapeDtypeStruct((WIDTH, BLK), BF16)
    full_turned = jax.ShapeDtypeStruct((WIDTH, BLK), F32)
    small = 2 * HEADS * BLK * HD * HD
    square = 2 * HEADS * BLK * BLK * HD
    keys_here, values_here, gain_here = (
        pltpu.with_memory_space_constraint(x, pltpu.HBM) for x in (keys, values, gain)
    )
    key_terms, gain = call(
        state_kernel,
        (state_shape, pltpu.VMEM((WIDTH,), BF16)),
        small,
        2**19,
        in_specs=[pl.BlockSpec(memory_space=pltpu.HBM)] * 3,
        scratch_shapes=[
            pltpu.VMEM((BLK, WIDTH), BF16),
            pltpu.VMEM((BLK, WIDTH), BF16),
            pltpu.SemaphoreType.DMA((3,)),
        ],
    )(keys_here, values_here, gain_here)
    pieces = exchange(key_terms.reshape(HALF, PIECE, HD), "seq", OWNERS_BEFORE)
    pieces = call(before_kernel, pltpu.VMEM((SEQ, PIECE, HD), F32), 2**16, 2**19)(pieces)
    key_parts = exchange(pieces, "seq", [BACK_BEFORE])
    attn, scaled, sums, key_state = call(
        attn_kernel,
        (
            full_turned,
            full_turned,
            jax.ShapeDtypeStruct((TP, 8, 128), F32),
            jax.ShapeDtypeStruct((WIDTH, HD), BF16),
        ),
        small + 2 * square,
        2**21,
    )(queries, keys, values, gain, grad_out, key_parts)
    sums = exchange(sums, "tp", [listed(TP, FIRST_TP)])
    grad_attn, query_terms = call(
        grad_kernel, (half_turned, pltpu.VMEM((SEQ, PIECE, HD), F32)), small, 2**21
    )(
        queries, scaled, attn, sums
    )
    pieces = exchange(query_terms, "seq", [OUT_AFTER])
    pieces = call(after_kernel, pltpu.VMEM((HALF, PIECE, HD), F32), 2**16, 2**19)(pieces)
    grad_state = exchange(pieces, "seq", OWNERS_AFTER).reshape(WIDTH, HD)
    grad_q, inner_k, inner_v = call(inner_kernel, (half, full, full), 6 * square, 2**22)(
        queries, keys, values, grad_attn, key_state
    )
    grad_k, grad_v = call(
        last_kernel,
        (half, half),
        2 * small,
        2**21,
        in_specs=[pl.BlockSpec(memory_space=pltpu.VMEM)] * 5,
        out_specs=(pl.BlockSpec(memory_space=pltpu.HBM),) * 2,
        scratch_shapes=[
            pltpu.VMEM((BLK, WIDTH), BF16),
            pltpu.VMEM((BLK, WIDTH), BF16),
            pltpu.SemaphoreType.DMA((2, BLK // TILE)),
        ],
    )(keys, values, inner_k, inner_v, grad_state)
    return grad_q, grad_k, grad_v


def solution(mesh):
    placed = (P("seq", "tp"), P("seq", "tp"), P("seq", "tp"), P("tp"), P("seq", "tp"))
    return jax.shard_map(
        local,
        mesh=mesh,
        in_specs=placed,
        out_specs=(P("seq", "tp"), P("seq", "tp"), P("seq", "tp")),
        check_vma=False,
    )
```

```python
import jax
import jax.numpy as jnp
from jax import lax
from jax.experimental import pallas as pl
from jax.experimental.pallas import tpu as pltpu
from jax.sharding import PartitionSpec as P

HD = 128
D = 4096
BLK = 512
TILE = 256
HEADS = 2
WIDTH = HEADS * HD
SEQ = 32
HALF = 16
PIECE = 32
PIECES = WIDTH // PIECE
TP = 16
EPSILON = 1e-06
LAST_TILES = 2
Z_A = 0
Z_B = 2
Z_C = 0
Z_D = 2
FIRST_A = 6
TURN_B = 8
TURN_C = 0
TURN_D = 0
FIRST_B = 10
FIRST_TP = 9
FIRST_C = 10
FIRST_D = 6

F32 = jnp.float32
BF16 = jnp.bfloat16


def nn(a, b):
    return lax.dot_general(a, b, (((1,), (0,)), ((), ())), preferred_element_type=F32)


def nt(a, b):
    return lax.dot_general(a, b, (((1,), (1,)), ((), ())), preferred_element_type=F32)


def tn(a, b):
    return lax.dot_general(a, b, (((0,), (0,)), ((), ())), preferred_element_type=F32)


def head(h):
    return slice(h * HD, (h + 1) * HD)


def tile(t):
    return slice(t * TILE, (t + 1) * TILE)


def masks():
    row = lax.broadcasted_iota(jnp.int32, (TILE, TILE), 0)
    col = lax.broadcasted_iota(jnp.int32, (TILE, TILE), 1)
    return col <= row, col >= row


def call(kernel, outs, flops, moved, limit=16, **spec):
    return pl.pallas_call(
        kernel,
        out_shape=outs,
        compiler_params=pltpu.CompilerParams(vmem_limit_bytes=limit * 2**20),
        cost_estimate=pl.CostEstimate(flops=flops, bytes_accessed=moved, transcendentals=0),
        **spec,
    )


def listed(size, first):
    return [(first + i) % size for i in range(size)]


def halves(z, first, turn=0):
    return [
        [(4 * z + half + i) % SEQ for i in listed(HALF, first + (turn if half else 0))]
        for half in (0, HALF)
    ]


OUT_BEFORE = halves(Z_A, FIRST_A)
BACK_BEFORE = halves(Z_B, FIRST_B, TURN_B)
OUT_AFTER = halves(Z_C, FIRST_C, TURN_C)
BACK_AFTER = halves(Z_D, FIRST_D, TURN_D)


def piece(block):
    return block % PIECES


def places(lists, p):
    return [i for i, block in enumerate(lists[0]) if piece(block) == p]


def own(lists, block):
    return lists[0] if block in lists[0] else lists[1]


def spread(terms, h, lists, out_ref):
    for i in range(HD // PIECE):
        for place in places(lists, h * (HD // PIECE) + i):
            out_ref[place] = terms[i * PIECE : (i + 1) * PIECE]


def joined(parts_ref, p, lists):
    first, second = places(lists, p)
    return parts_ref[first] + parts_ref[second]


def state_kernel(k_hbm, v_hbm, gain_hbm, out_ref, gain_ref, k_ref, v_ref, sems):
    copies = (
        pltpu.make_async_copy(v_hbm, v_ref, sems.at[0]),
        pltpu.make_async_copy(k_hbm, k_ref, sems.at[1]),
        pltpu.make_async_copy(gain_hbm, gain_ref, sems.at[2]),
    )
    for copy in copies:
        copy.start()
    copies[0].wait()
    turned = [v_ref[:, head(h)].T for h in range(HEADS)]
    copies[1].wait()
    for h in range(HEADS):
        spread(nn(turned[h], k_ref[:, head(h)]), h, OUT_BEFORE, out_ref)
    copies[2].wait()


def running_sums(blocks, out, back, in_ref, out_ref):
    for pair in range(SEQ // PIECES):

        @pl.when(lax.div(lax.axis_index("seq"), PIECES) == pair)
        def _():
            senders, receivers = own(out, pair * PIECES), own(back, pair * PIECES)
            acc = jnp.zeros((PIECE, 128), F32)
            for b in blocks:
                if b in receivers:
                    out_ref[receivers.index(b)] = acc
                if b in senders:
                    acc = acc + in_ref[senders.index(b)]


def before_kernel(in_ref, out_ref):
    running_sums(range(SEQ), OUT_BEFORE, BACK_BEFORE, in_ref, out_ref)


def after_kernel(in_ref, out_ref):
    running_sums(range(SEQ - 1, -1, -1), OUT_AFTER, BACK_AFTER, in_ref, out_ref)


def attn_kernel(q_ref, k_ref, v_ref, gain_ref, go_ref, parts_ref, attn_ref, scaled_ref, sums_ref, state_ref):
    for p in range(PIECES):
        state_ref[p * PIECE : (p + 1) * PIECE, :] = joined(parts_ref, p, BACK_BEFORE).astype(BF16)
    _, upper = masks()
    gain = jnp.broadcast_to(gain_ref[...].astype(F32)[None, :], (8, WIDTH)).T[:, 0:1]
    square = [jnp.zeros((8, TILE), F32) for _ in range(BLK // TILE)]
    cross = [jnp.zeros((8, TILE), F32) for _ in range(BLK // TILE)]
    for h in range(HEADS):
        state = state_ref[head(h), :]
        v = v_ref[:, head(h)].T
        scaled_ref[head(h), :] = go_ref[:, head(h)].T.astype(F32) * gain[head(h)]
        for t in range(BLK // TILE):
            q = q_ref[tile(t), head(h)]
            attn = nt(state, q)
            for s in range(t + 1):
                scores = nt(k_ref[tile(s), head(h)], q)
                if s == t:
                    scores = jnp.where(upper, scores, 0.0)
                attn = attn + nn(v[:, tile(s)], scores.astype(BF16))
            attn_ref[head(h), tile(t)] = attn
            scaled = scaled_ref[head(h), tile(t)]
            square[t] = square[t] + jnp.sum((attn * attn).reshape(HD // 8, 8, TILE), axis=0)
            cross[t] = cross[t] + jnp.sum((scaled * attn).reshape(HD // 8, 8, TILE), axis=0)
    rows = []
    for kind in (square, cross):
        for part in kind:
            row = jnp.sum(part, axis=0, keepdims=True)
            rows += [row[:, i * 128 : (i + 1) * 128] for i in range(TILE // 128)]
    sums_ref[...] = jnp.broadcast_to(jnp.concatenate(rows, axis=0)[None], (TP, 8, 128))


def grad_kernel(q_ref, scaled_ref, attn_ref, sums_ref, g_ref, out_ref):
    total = jnp.sum(sums_ref[...], axis=0)
    inv = lax.rsqrt(total[0:4] / D + EPSILON)
    factor = total[4:8] * (inv * inv * inv) / D
    inv = jnp.concatenate([inv[i : i + 1] for i in range(BLK // 128)], axis=1)
    factor = jnp.concatenate([factor[i : i + 1] for i in range(BLK // 128)], axis=1)
    for h in range(HEADS):
        g = (scaled_ref[head(h), :] * inv - attn_ref[head(h), :] * factor).astype(BF16)
        g_ref[head(h), :] = g
        spread(nn(g, q_ref[:, head(h)]), h, OUT_AFTER, out_ref)


def inner_kernel(q_ref, k_ref, v_ref, g_ref, state_ref, gq_ref, gk_ref, gv_ref):
    lower, upper = masks()
    for h in range(HEADS):
        g = g_ref[head(h), :].T
        state = state_ref[head(h), :]
        for t in range(BLK // TILE):
            grad = nn(g[tile(t)], state)
            for s in range(t + 1):
                scores = nt(g[tile(t)], v_ref[tile(s), head(h)])
                if s == t:
                    scores = jnp.where(lower, scores, 0.0)
                grad = grad + nn(scores.astype(BF16), k_ref[tile(s), head(h)])
            gq_ref[tile(t), head(h)] = grad.astype(BF16)
        for s in range(BLK // TILE):
            gk = gv = None
            for t in range(s, BLK // TILE):
                q = q_ref[tile(t), head(h)]
                scores = nt(k_ref[tile(s), head(h)], q)
                grads = nn(v_ref[tile(s), head(h)], g_ref[head(h), tile(t)])
                if s == t:
                    scores = jnp.where(upper, scores, 0.0)
                    grads = jnp.where(upper, grads, 0.0)
                gk_term = nn(grads.astype(BF16), q)
                gv_term = nn(scores.astype(BF16), g[tile(t)])
                gk = gk_term if gk is None else gk + gk_term
                gv = gv_term if gv is None else gv + gv_term
            gk_ref[tile(s), head(h)] = gk
            gv_ref[tile(s), head(h)] = gv


def last_kernel(k_ref, v_ref, gk_in_ref, gv_in_ref, parts_ref, gk_hbm, gv_hbm, gk_ref, gv_ref, sems):
    parts = [joined(parts_ref, p, BACK_AFTER).astype(BF16) for p in range(PIECES)]
    state = [jnp.concatenate(parts[h * PIECES // 2 : (h + 1) * PIECES // 2], axis=0) for h in range(HEADS)]
    copies = []
    for t in range(LAST_TILES):
        rows = slice(t * BLK // LAST_TILES, (t + 1) * BLK // LAST_TILES)
        for i, (mine, out) in enumerate(((gk_ref, gk_hbm), (gv_ref, gv_hbm))):
            for h in range(HEADS):
                if i == 0:
                    grad = gk_in_ref[rows, head(h)] + nn(v_ref[rows, head(h)], state[h])
                else:
                    grad = gv_in_ref[rows, head(h)] + nt(k_ref[rows, head(h)], state[h])
                mine[rows, head(h)] = grad.astype(BF16)
            copies.append(pltpu.make_async_copy(mine.at[rows], out.at[rows], sems.at[i, t]))
            copies[-1].start()
    for copy in copies:
        copy.wait()


def exchange(pieces, axis, groups):
    return lax.all_to_all(pieces, axis, 0, 0, tiled=True, axis_index_groups=groups)


def local(queries, keys, values, gain, grad_out):
    piece_shape = pltpu.VMEM((HALF, PIECE, HD), F32)
    half = jax.ShapeDtypeStruct((BLK, WIDTH), BF16)
    full = jax.ShapeDtypeStruct((BLK, WIDTH), F32)
    half_turned = jax.ShapeDtypeStruct((WIDTH, BLK), BF16)
    full_turned = jax.ShapeDtypeStruct((WIDTH, BLK), F32)
    small = 2 * HEADS * BLK * HD * HD
    square = 2 * HEADS * BLK * BLK * HD
    keys_here, values_here, gain_here = (
        pltpu.with_memory_space_constraint(x, pltpu.HBM) for x in (keys, values, gain)
    )
    key_terms, gain = call(
        state_kernel,
        (piece_shape, pltpu.VMEM((WIDTH,), BF16)),
        small,
        2**19,
        in_specs=[pl.BlockSpec(memory_space=pltpu.HBM)] * 3,
        scratch_shapes=[
            pltpu.VMEM((BLK, WIDTH), BF16),
            pltpu.VMEM((BLK, WIDTH), BF16),
            pltpu.SemaphoreType.DMA((3,)),
        ],
    )(keys_here, values_here, gain_here)
    pieces = exchange(key_terms, "seq", OUT_BEFORE)
    pieces = call(before_kernel, piece_shape, 2**16, 2**19)(pieces)
    key_parts = exchange(pieces, "seq", BACK_BEFORE)
    attn, scaled, sums, key_state = call(
        attn_kernel,
        (
            full_turned,
            full_turned,
            jax.ShapeDtypeStruct((TP, 8, 128), F32),
            jax.ShapeDtypeStruct((WIDTH, HD), BF16),
        ),
        small + 2 * square,
        2**21,
    )(queries, keys, values, gain, grad_out, key_parts)
    sums = exchange(sums, "tp", [listed(TP, FIRST_TP)])
    grad_attn, query_terms = call(
        grad_kernel, (half_turned, piece_shape), small, 2**21
    )(
        queries, scaled, attn, sums
    )
    pieces = exchange(query_terms, "seq", OUT_AFTER)
    pieces = call(after_kernel, piece_shape, 2**16, 2**19)(pieces)
    grad_parts = exchange(pieces, "seq", BACK_AFTER)
    grad_q, inner_k, inner_v = call(inner_kernel, (half, full, full), 6 * square, 2**22)(
        queries, keys, values, grad_attn, key_state
    )
    grad_k, grad_v = call(
        last_kernel,
        (half, half),
        2 * small,
        2**21,
        in_specs=[pl.BlockSpec(memory_space=pltpu.VMEM)] * 5,
        out_specs=(pl.BlockSpec(memory_space=pltpu.HBM),) * 2,
        scratch_shapes=[
            pltpu.VMEM((BLK, WIDTH), BF16),
            pltpu.VMEM((BLK, WIDTH), BF16),
            pltpu.SemaphoreType.DMA((2, LAST_TILES)),
        ],
    )(keys, values, inner_k, inner_v, grad_parts)
    return grad_q, grad_k, grad_v


def solution(mesh):
    placed = (P("seq", "tp"), P("seq", "tp"), P("seq", "tp"), P("tp"), P("seq", "tp"))
    return jax.shard_map(
        local,
        mesh=mesh,
        in_specs=placed,
        out_specs=(P("seq", "tp"), P("seq", "tp"), P("seq", "tp")),
        check_vma=False,
    )
```

```python
import jax
import jax.numpy as jnp
from jax import lax
from jax.experimental import pallas as pl
from jax.experimental.pallas import tpu as pltpu
from jax.sharding import PartitionSpec as P

HD = 128
D = 4096
BLK = 512
TILE = 256
HEADS = 2
WIDTH = HEADS * HD
SEQ = 32
HALF = 16
PIECE_BEFORE = 16
PIECE = 32
PIECES = WIDTH // PIECE
TP = 16
EPSILON = 1e-06
LAST_TILES = 2
Z_A = 0
Z_C = 0
Z_D = 2
FIRST_A = 6
TURN_C = 0
TURN_D = 0
FIRST_B = 22
FIRST_TP = 9
FIRST_C = 10
FIRST_D = 6

F32 = jnp.float32
BF16 = jnp.bfloat16


def nn(a, b):
    return lax.dot_general(a, b, (((1,), (0,)), ((), ())), preferred_element_type=F32)


def nt(a, b):
    return lax.dot_general(a, b, (((1,), (1,)), ((), ())), preferred_element_type=F32)


def tn(a, b):
    return lax.dot_general(a, b, (((0,), (0,)), ((), ())), preferred_element_type=F32)


def head(h):
    return slice(h * HD, (h + 1) * HD)


def tile(t):
    return slice(t * TILE, (t + 1) * TILE)


def masks():
    row = lax.broadcasted_iota(jnp.int32, (TILE, TILE), 0)
    col = lax.broadcasted_iota(jnp.int32, (TILE, TILE), 1)
    return col <= row, col >= row


def call(kernel, outs, flops, moved, limit=16, **spec):
    return pl.pallas_call(
        kernel,
        out_shape=outs,
        compiler_params=pltpu.CompilerParams(vmem_limit_bytes=limit * 2**20),
        cost_estimate=pl.CostEstimate(flops=flops, bytes_accessed=moved, transcendentals=0),
        **spec,
    )


def listed(size, first):
    return [(first + i) % size for i in range(size)]


def halves(z, first, turn=0):
    return [
        [(4 * z + half + i) % SEQ for i in listed(HALF, first + (turn if half else 0))]
        for half in (0, HALF)
    ]


OUT_BEFORE = halves(Z_A, FIRST_A)
BACK_BEFORE = listed(SEQ, FIRST_B)
OUT_AFTER = halves(Z_C, FIRST_C, TURN_C)
BACK_AFTER = halves(Z_D, FIRST_D, TURN_D)


def piece(block):
    return block % PIECES


def places(lists, p):
    return [i for i, block in enumerate(lists[0]) if piece(block) == p]


def own(lists, block):
    return lists[0] if block in lists[0] else lists[1]


def spread(terms, h, lists, out_ref):
    for i in range(HD // PIECE):
        for place in places(lists, h * (HD // PIECE) + i):
            out_ref[place] = terms[i * PIECE : (i + 1) * PIECE]


def joined(parts_ref, p, lists):
    first, second = places(lists, p)
    return parts_ref[first] + parts_ref[second]


def state_kernel(k_hbm, v_hbm, gain_hbm, out_ref, gain_ref, k_ref, v_ref, sems):
    copies = (
        pltpu.make_async_copy(v_hbm, v_ref, sems.at[0]),
        pltpu.make_async_copy(k_hbm, k_ref, sems.at[1]),
        pltpu.make_async_copy(gain_hbm, gain_ref, sems.at[2]),
    )
    for copy in copies:
        copy.start()
    copies[0].wait()
    turned = [v_ref[:, head(h)].T for h in range(HEADS)]
    copies[1].wait()
    for h in range(HEADS):
        terms = nn(turned[h], k_ref[:, head(h)])
        for i in range(HD // PIECE_BEFORE):
            out_ref[h * (HD // PIECE_BEFORE) + i] = terms[i * PIECE_BEFORE : (i + 1) * PIECE_BEFORE]
    copies[2].wait()


def running_sums(blocks, out, back, in_ref, out_ref):
    for pair in range(SEQ // PIECES):

        @pl.when(lax.div(lax.axis_index("seq"), PIECES) == pair)
        def _():
            senders, receivers = own(out, pair * PIECES), own(back, pair * PIECES)
            acc = jnp.zeros((PIECE, 128), F32)
            for b in blocks:
                if b in receivers:
                    out_ref[receivers.index(b)] = acc
                if b in senders:
                    acc = acc + in_ref[senders.index(b)]


def before_kernel(in_ref, out_ref):
    place = lax.rem(lax.axis_index("seq") + (SEQ - 4 * Z_A), SEQ)
    for half, owners in enumerate(OUT_BEFORE):

        @pl.when(lax.div(place, HALF) == half)
        def _():
            acc = jnp.zeros((PIECE_BEFORE, 128), F32)
            for b in range(SEQ):
                out_ref[BACK_BEFORE.index(b)] = acc
                if b in owners:
                    acc = acc + in_ref[owners.index(b)]


def after_kernel(in_ref, out_ref):
    running_sums(range(SEQ - 1, -1, -1), OUT_AFTER, BACK_AFTER, in_ref, out_ref)


def attn_kernel(q_ref, k_ref, v_ref, gain_ref, go_ref, parts_ref, attn_ref, scaled_ref, sums_ref, state_ref):
    for i, owners in enumerate(zip(*OUT_BEFORE)):
        part = sum(parts_ref[BACK_BEFORE.index(owner)] for owner in owners)
        state_ref[i * PIECE_BEFORE : (i + 1) * PIECE_BEFORE, :] = part.astype(BF16)
    _, upper = masks()
    gain = jnp.broadcast_to(gain_ref[...].astype(F32)[None, :], (8, WIDTH)).T[:, 0:1]
    square = [jnp.zeros((8, TILE), F32) for _ in range(BLK // TILE)]
    cross = [jnp.zeros((8, TILE), F32) for _ in range(BLK // TILE)]
    for h in range(HEADS):
        state = state_ref[head(h), :]
        v = v_ref[:, head(h)].T
        scaled_ref[head(h), :] = go_ref[:, head(h)].T.astype(F32) * gain[head(h)]
        for t in range(BLK // TILE):
            q = q_ref[tile(t), head(h)]
            attn = nt(state, q)
            for s in range(t + 1):
                scores = nt(k_ref[tile(s), head(h)], q)
                if s == t:
                    scores = jnp.where(upper, scores, 0.0)
                attn = attn + nn(v[:, tile(s)], scores.astype(BF16))
            attn_ref[head(h), tile(t)] = attn
            scaled = scaled_ref[head(h), tile(t)]
            square[t] = square[t] + jnp.sum((attn * attn).reshape(HD // 8, 8, TILE), axis=0)
            cross[t] = cross[t] + jnp.sum((scaled * attn).reshape(HD // 8, 8, TILE), axis=0)
    rows = []
    for kind in (square, cross):
        for part in kind:
            row = jnp.sum(part, axis=0, keepdims=True)
            rows += [row[:, i * 128 : (i + 1) * 128] for i in range(TILE // 128)]
    sums_ref[...] = jnp.broadcast_to(jnp.concatenate(rows, axis=0)[None], (TP, 8, 128))


def grad_kernel(q_ref, scaled_ref, attn_ref, sums_ref, g_ref, out_ref):
    total = jnp.sum(sums_ref[...], axis=0)
    inv = lax.rsqrt(total[0:4] / D + EPSILON)
    factor = total[4:8] * (inv * inv * inv) / D
    inv = jnp.concatenate([inv[i : i + 1] for i in range(BLK // 128)], axis=1)
    factor = jnp.concatenate([factor[i : i + 1] for i in range(BLK // 128)], axis=1)
    for h in range(HEADS):
        g = (scaled_ref[head(h), :] * inv - attn_ref[head(h), :] * factor).astype(BF16)
        g_ref[head(h), :] = g
        spread(nn(g, q_ref[:, head(h)]), h, OUT_AFTER, out_ref)


def inner_kernel(q_ref, k_ref, v_ref, g_ref, state_ref, gq_ref, gk_ref, gv_ref):
    lower, upper = masks()
    for h in range(HEADS):
        g = g_ref[head(h), :].T
        state = state_ref[head(h), :]
        for t in range(BLK // TILE):
            grad = nn(g[tile(t)], state)
            for s in range(t + 1):
                scores = nt(g[tile(t)], v_ref[tile(s), head(h)])
                if s == t:
                    scores = jnp.where(lower, scores, 0.0)
                grad = grad + nn(scores.astype(BF16), k_ref[tile(s), head(h)])
            gq_ref[tile(t), head(h)] = grad.astype(BF16)
        for s in range(BLK // TILE):
            gk = gv = None
            for t in range(s, BLK // TILE):
                q = q_ref[tile(t), head(h)]
                scores = nt(k_ref[tile(s), head(h)], q)
                grads = nn(v_ref[tile(s), head(h)], g_ref[head(h), tile(t)])
                if s == t:
                    scores = jnp.where(upper, scores, 0.0)
                    grads = jnp.where(upper, grads, 0.0)
                gk_term = nn(grads.astype(BF16), q)
                gv_term = nn(scores.astype(BF16), g[tile(t)])
                gk = gk_term if gk is None else gk + gk_term
                gv = gv_term if gv is None else gv + gv_term
            gk_ref[tile(s), head(h)] = gk
            gv_ref[tile(s), head(h)] = gv


def last_kernel(k_ref, v_ref, gk_in_ref, gv_in_ref, parts_ref, gk_hbm, gv_hbm, gk_ref, gv_ref, sems):
    parts = [joined(parts_ref, p, BACK_AFTER).astype(BF16) for p in range(PIECES)]
    state = [jnp.concatenate(parts[h * PIECES // 2 : (h + 1) * PIECES // 2], axis=0) for h in range(HEADS)]
    copies = []
    for t in range(LAST_TILES):
        rows = slice(t * BLK // LAST_TILES, (t + 1) * BLK // LAST_TILES)
        for i, (mine, out) in enumerate(((gk_ref, gk_hbm), (gv_ref, gv_hbm))):
            for h in range(HEADS):
                if i == 0:
                    grad = gk_in_ref[rows, head(h)] + nn(v_ref[rows, head(h)], state[h])
                else:
                    grad = gv_in_ref[rows, head(h)] + nt(k_ref[rows, head(h)], state[h])
                mine[rows, head(h)] = grad.astype(BF16)
            copies.append(pltpu.make_async_copy(mine.at[rows], out.at[rows], sems.at[i, t]))
            copies[-1].start()
    for copy in copies:
        copy.wait()


def exchange(pieces, axis, groups):
    return lax.all_to_all(pieces, axis, 0, 0, tiled=True, axis_index_groups=groups)


def local(queries, keys, values, gain, grad_out):
    piece_shape = pltpu.VMEM((HALF, PIECE, HD), F32)
    half = jax.ShapeDtypeStruct((BLK, WIDTH), BF16)
    full = jax.ShapeDtypeStruct((BLK, WIDTH), F32)
    half_turned = jax.ShapeDtypeStruct((WIDTH, BLK), BF16)
    full_turned = jax.ShapeDtypeStruct((WIDTH, BLK), F32)
    small = 2 * HEADS * BLK * HD * HD
    square = 2 * HEADS * BLK * BLK * HD
    keys_here, values_here, gain_here = (
        pltpu.with_memory_space_constraint(x, pltpu.HBM) for x in (keys, values, gain)
    )
    key_terms, gain = call(
        state_kernel,
        (pltpu.VMEM((HALF, PIECE_BEFORE, HD), F32), pltpu.VMEM((WIDTH,), BF16)),
        small,
        2**19,
        in_specs=[pl.BlockSpec(memory_space=pltpu.HBM)] * 3,
        scratch_shapes=[
            pltpu.VMEM((BLK, WIDTH), BF16),
            pltpu.VMEM((BLK, WIDTH), BF16),
            pltpu.SemaphoreType.DMA((3,)),
        ],
    )(keys_here, values_here, gain_here)
    pieces = exchange(key_terms, "seq", OUT_BEFORE)
    sums_shape = pltpu.VMEM((SEQ, PIECE_BEFORE, HD), F32)
    pieces = call(before_kernel, sums_shape, 2**16, 2**19)(pieces)
    key_parts = exchange(pieces, "seq", [BACK_BEFORE])
    attn, scaled, sums, key_state = call(
        attn_kernel,
        (
            full_turned,
            full_turned,
            jax.ShapeDtypeStruct((TP, 8, 128), F32),
            jax.ShapeDtypeStruct((WIDTH, HD), BF16),
        ),
        small + 2 * square,
        2**21,
    )(queries, keys, values, gain, grad_out, key_parts)
    sums = exchange(sums, "tp", [listed(TP, FIRST_TP)])
    grad_attn, query_terms = call(
        grad_kernel, (half_turned, piece_shape), small, 2**21
    )(
        queries, scaled, attn, sums
    )
    pieces = exchange(query_terms, "seq", OUT_AFTER)
    pieces = call(after_kernel, piece_shape, 2**16, 2**19)(pieces)
    grad_parts = exchange(pieces, "seq", BACK_AFTER)
    grad_q, inner_k, inner_v = call(inner_kernel, (half, full, full), 6 * square, 2**22)(
        queries, keys, values, grad_attn, key_state
    )
    grad_k, grad_v = call(
        last_kernel,
        (half, half),
        2 * small,
        2**21,
        in_specs=[pl.BlockSpec(memory_space=pltpu.VMEM)] * 5,
        out_specs=(pl.BlockSpec(memory_space=pltpu.HBM),) * 2,
        scratch_shapes=[
            pltpu.VMEM((BLK, WIDTH), BF16),
            pltpu.VMEM((BLK, WIDTH), BF16),
            pltpu.SemaphoreType.DMA((2, LAST_TILES)),
        ],
    )(keys, values, inner_k, inner_v, grad_parts)
    return grad_q, grad_k, grad_v


def solution(mesh):
    placed = (P("seq", "tp"), P("seq", "tp"), P("seq", "tp"), P("tp"), P("seq", "tp"))
    return jax.shard_map(
        local,
        mesh=mesh,
        in_specs=placed,
        out_specs=(P("seq", "tp"), P("seq", "tp"), P("seq", "tp")),
        check_vma=False,
    )
```
